32 devices in a mesh: col: 8 (over z, y), row: 4 (over x, core).
Axes of the slice: x: 2, y: 2, z: 4, core: 2. Of those that a mesh axis runs over, the one named last changes fastest.
Arguments:
- q_left: bfloat16 [4096, 4096], P('row'), may hold values from -2 to 2, as said below
- grad: bfloat16 [4096, 14336], P('row', 'col'), may hold values from -250 to 250
- q_right: float32 [14336], P('col'), may hold values from 0.5 to 2
Outputs:
- new_left: float32 [4096, 4096], P('row', 'col')
- precond: bfloat16 [4096, 14336], P('row', 'col')
The draws below stay inside these ranges and needn't reach their ends.
Inputs may be any that keep to these rules, and one draw needn't show every extreme that they name: `q_left`: a diagonal of positive entries with dense off-diagonal entries.
All inputs are finite; a program needn't handle non-finite values.
Results may differ from the reference program's by a relative error of at most 0.0045.
Values may be sent and summed in bfloat16 or wider, within the bound.
A program may use at most 192 MiB of HBM per device.

```python
import math
import jax
import jax.numpy as jnp

M = 4096
N = 14336


def draw_q_left(key, part):
    key = jax.random.fold_in(key, 11)
    key_diag, key_off = jax.random.split(key)
    diag_vals = jnp.exp(jax.random.uniform(key_diag, (M,), jnp.float32, jnp.log(0.6), jnp.log(1.6)))
    off = jnp.clip(jax.random.normal(key_off, (M, M), jnp.float32), -6.0, 6.0)
    off = off * (0.5 / jnp.sqrt(jnp.float32(M)))
    eye_mat = jnp.eye(M, dtype=jnp.float32)
    return (off * (1.0 - eye_mat) + eye_mat * diag_vals[:, None]).astype(jnp.bfloat16)


def draw_grad(key, part):
    key = jax.random.fold_in(key, 23)
    key_z, key_r, key_c = jax.random.split(key, 3)
    ramp = jnp.exp(jnp.log(3.0) * jnp.arange(N, dtype=jnp.float32) / N)
    col_scale = jnp.exp(jax.random.uniform(key_c, (N,), jnp.float32, 0.0, jnp.log(3.2))) * ramp
    row_scale = jnp.exp(jax.random.uniform(key_r, (M,), jnp.float32, 0.0, jnp.log(3.2)))
    base = jnp.clip(jax.random.normal(key_z, (M, N), jnp.float32), -6.0, 6.0)
    return (base * row_scale[:, None] * col_scale[None, :]).astype(jnp.bfloat16)


def shard_levels(stream_key, dims, pieces, low, high):
    def one(position, parts):
        heights = jax.random.uniform(jax.random.fold_in(jax.random.fold_in(stream_key, 6), position), (parts,), jnp.float32, low / len(pieces), high / len(pieces))
        return jnp.repeat(jnp.exp(heights), dims[position] // parts).reshape((-1,) + (1,) * (len(dims) - position - 1))

    gain = one(*pieces[0])
    for cut in pieces[1:]:
        gain = gain * one(*cut)
    return gain


def setup_inputs(seed: int = 0) -> dict:
    key_of = jax.random.split(jax.random.key(seed), 4)
    return {
        "q_left": draw_q_left(jax.random.fold_in(key_of[3], 71), 0),
        "grad": draw_grad(jax.random.fold_in(key_of[3], 71), 0),
        "q_right": jnp.clip(jnp.exp(math.log(2.0) - 1.3862944 * jax.random.uniform(key_of[2], (N,), jnp.float32) ** shard_levels(key_of[2], (N,), ((0, 8),), -0.2, 0.2)), 0.5, 2.0),
    }


step_rate = 0.5
epsilon = 1e-6


def reference(q_left, grad, q_right):
    acc = jnp.dot(q_left, grad, preferred_element_type=jnp.float32)
    act = (acc * q_right[None, :]).astype(jnp.bfloat16)
    act_f = act.astype(jnp.float32)
    scale = jnp.sum(act_f * act_f) / M + epsilon
    gram = jnp.dot(act, act.T, preferred_element_type=jnp.float32)
    gram_b = gram.astype(jnp.bfloat16)
    upper = jnp.triu(gram_b)
    stepped = jnp.dot(upper, q_left, preferred_element_type=jnp.float32)
    q_full = q_left.astype(jnp.float32)
    new_left = q_full - step_rate * (stepped / scale - q_full)
    pre = jnp.dot(q_left.T, act, preferred_element_type=jnp.float32)
    precond = (pre * q_right[None, :]).astype(jnp.bfloat16)
    return new_left, precond
```

```python
import jax
import jax.numpy as jnp
from jax import lax
from jax.sharding import PartitionSpec as P

step_rate = 0.5
epsilon = 1e-06
f32 = jnp.float32
bf16 = jnp.bfloat16


def dot_nn(a, b):
    return lax.dot_general(a, b, (((1,), (0,)), ((), ())), preferred_element_type=f32)


def dot_nt(a, b):
    return lax.dot_general(a, b, (((1,), (1,)), ((), ())), preferred_element_type=f32)


def dot_tn(a, b):
    return lax.dot_general(a, b, (((0,), (0,)), ((), ())), preferred_element_type=f32)


def swap(x, by):
    return lax.ppermute(x, "row", [(i, i ^ by) for i in range(4)])


def shards(q_left, grad, q_right):
    rows, order = q_left.shape
    r = lax.axis_index("row")
    c = lax.axis_index("col")
    col_count = lax.axis_size("col")
    assert lax.axis_size("row") == 4
    piece = rows // col_count
    width = order // col_count
    half = rows // 2

    grad_all = lax.all_gather(grad, "row", axis=0, tiled=True)
    q_far_piece = swap(lax.dynamic_slice_in_dim(q_left, c * piece, piece, 0), 2)
    q_far = lax.all_gather(q_far_piece, "col", axis=0, tiled=True)
    q_mate = swap(q_left, 1)
    q_far_mate = swap(q_far, 1)

    def act_of(q):
        return (dot_nn(q, grad_all) * q_right[None, :]).astype(bf16)

    own = act_of(q_left)
    far = act_of(q_far)
    mate = swap(own, 1)
    far_mate = swap(far, 1)

    own_f = own.astype(f32)
    total_sq = lax.psum(jnp.sum(own_f * own_f), ("col", "row"))
    scale = total_sq / order + epsilon

    even = (r % 2) == 0
    lhs2 = jnp.where(r == 3, far_mate, own)
    rhs2 = jnp.where(even, mate, jnp.where(r == 3, own, far_mate))
    lhs3 = jnp.where(r >= 2, far, own)
    rhs3 = jnp.where(r >= 2, own[half:], far[:half])
    part = jnp.concatenate(
        [dot_nt(own, own).astype(bf16), dot_nt(lhs2, rhs2).astype(bf16), dot_nt(lhs3, rhs3).astype(bf16)],
        axis=1,
    )
    gram = lax.psum_scatter(part, "col", scatter_dimension=0, tiled=True)
    p1 = gram[:, :rows]
    p2 = gram[:, rows : 2 * rows]
    p3 = gram[:, 2 * rows :]
    got2 = lax.ppermute(p2, "row", [(3, 0)])
    got3 = lax.ppermute(p3, "row", [(2, 0), (3, 1)])
    zero = jnp.zeros_like(p1)
    row_ids = c * piece + lax.broadcasted_iota(jnp.int32, p1.shape, 0)
    col_ids = lax.broadcasted_iota(jnp.int32, p1.shape, 1)
    upper = jnp.concatenate(
        [
            jnp.where(col_ids >= row_ids, p1, zero),
            jnp.where(even, p2, zero),
            jnp.where(r < 2, jnp.concatenate([p3, got3], axis=1), zero),
            jnp.where(r == 0, got2, jnp.where(r == 1, p2, zero)),
        ],
        axis=1,
    )
    q_all = jnp.concatenate([q_left, q_mate, q_far, q_far_mate], axis=0)
    ratio = (dot_nn(upper, q_all) / scale).astype(bf16)
    ratio = lax.all_to_all(ratio, "col", split_axis=1, concat_axis=0, tiled=True)
    q_tile = lax.dynamic_slice_in_dim(q_left, c * width, width, 1).astype(f32)
    new_left = q_tile - step_rate * (ratio.astype(f32) - q_tile)

    q_cols = lax.dynamic_slice_in_dim(q_all, r * rows, rows, 1)
    act_all = jnp.concatenate([own, mate, far, far_mate], axis=0)
    precond = (dot_tn(q_cols, act_all) * q_right[None, :]).astype(bf16)
    return (new_left, precond)


def solution(mesh):
    in_specs = (P("row", None), P("row", "col"), P("col"))
    out_specs = (P("row", "col"), P("row", "col"))
    return jax.shard_map(shards, mesh=mesh, in_specs=in_specs, out_specs=out_specs, check_vma=False)
```

```python
import jax
import jax.numpy as jnp
from jax import lax
from jax.sharding import PartitionSpec as P

step_rate = 0.5
epsilon = 1e-06
f32 = jnp.float32
bf16 = jnp.bfloat16


def dot_nn(a, b):
    return lax.dot_general(a, b, (((1,), (0,)), ((), ())), preferred_element_type=f32)


def dot_nt(a, b):
    return lax.dot_general(a, b, (((1,), (1,)), ((), ())), preferred_element_type=f32)


def dot_tn(a, b):
    return lax.dot_general(a, b, (((0,), (0,)), ((), ())), preferred_element_type=f32)


def swap(x, by):
    return lax.ppermute(x, "row", [(i, i ^ by) for i in range(4)])


def shards(q_left, grad, q_right):
    rows, order = q_left.shape
    r = lax.axis_index("row")
    c = lax.axis_index("col")
    col_count = lax.axis_size("col")
    assert lax.axis_size("row") == 4
    piece = rows // col_count
    width = order // col_count
    half = rows // 2

    def far_half(p):
        mine = lax.dynamic_slice_in_dim(q_left, p * half + c * (piece // 2), piece // 2, 0)
        return lax.all_gather(swap(mine, 2), "col", axis=0, tiled=True)

    q_far0 = far_half(0)
    q_far1 = far_half(1)
    grad_far = swap(grad, 2)
    grad_mate = swap(grad, 1)
    grad_far_mate = swap(grad_far, 1)
    grad_all = jnp.zeros((order,) + grad.shape[1:], grad.dtype)
    for by, block in ((0, grad), (1, grad_mate), (2, grad_far), (3, grad_far_mate)):
        grad_all = lax.dynamic_update_slice_in_dim(grad_all, block, (r ^ by) * rows, 0)
    q_mate = swap(q_left, 1)
    q_far_mate0 = swap(q_far0, 1)
    q_far_mate1 = swap(q_far1, 1)

    def act_of(q):
        return (dot_nn(q, grad_all) * q_right[None, :]).astype(bf16)

    own = act_of(q_left)
    mate = swap(own, 1)
    far0 = act_of(q_far0)
    far_mate0 = swap(far0, 1)
    far1 = act_of(q_far1)
    far_mate1 = swap(far1, 1)
    far = jnp.concatenate([far0, far1], axis=0)
    far_mate = jnp.concatenate([far_mate0, far_mate1], axis=0)

    own_f = own.astype(f32)
    total_sq = jnp.sum(own_f * own_f).reshape(1, 1)
    total_sq = total_sq + swap(total_sq, 1)
    total_sq = total_sq + swap(total_sq, 2)
    by = 1
    while by < col_count:
        total_sq = total_sq + lax.ppermute(total_sq, "col", [(i, i ^ by) for i in range(col_count)])
        by *= 2
    scale = total_sq / order + epsilon

    even = (r % 2) == 0
    lhs2 = jnp.where(r == 3, far_mate, own)
    rhs2 = jnp.where(even, mate, jnp.where(r == 3, own, far_mate))
    lhs3 = jnp.where(r >= 2, far, own)
    rhs3 = jnp.where(r >= 2, own[half:], far0)

    def col_sum(a, b):
        return lax.psum_scatter(dot_nt(a, b).astype(bf16), "col", scatter_dimension=0, tiled=True)

    p1 = col_sum(own, own)
    p3 = col_sum(lhs3, rhs3)
    p2 = col_sum(lhs2, rhs2)

    q_all = jnp.concatenate(
        [q_left, q_mate, q_far0, q_far1, q_far_mate0, q_far_mate1], axis=0
    )
    q_cols = lax.dynamic_slice_in_dim(q_all, r * rows, rows, 1)
    act_all = jnp.concatenate([own, mate, far, far_mate], axis=0)
    precond = (dot_tn(q_cols, act_all) * q_right[None, :]).astype(bf16)
    p2, precond = lax.optimization_barrier((p2, precond))

    got3 = lax.ppermute(p3, "row", [(2, 0), (3, 1)])
    got2 = lax.ppermute(p2, "row", [(3, 0)])
    zero = jnp.zeros_like(p1)
    row_ids = c * piece + lax.broadcasted_iota(jnp.int32, p1.shape, 0)
    col_ids = lax.broadcasted_iota(jnp.int32, p1.shape, 1)
    upper = jnp.concatenate(
        [
            jnp.where(col_ids >= row_ids, p1, zero),
            jnp.where(even, p2, zero),
            jnp.where(r < 2, jnp.concatenate([p3, got3], axis=1), zero),
            jnp.where(r == 0, got2, jnp.where(r == 1, p2, zero)),
        ],
        axis=1,
    )
    ratio = (dot_nn(upper, q_all) / scale).astype(bf16)
    ratio = lax.all_to_all(ratio, "col", split_axis=1, concat_axis=0, tiled=True)
    q_tile = lax.dynamic_slice_in_dim(q_left, c * width, width, 1).astype(f32)
    new_left = q_tile - step_rate * (ratio.astype(f32) - q_tile)
    return (new_left, precond)


def solution(mesh):
    in_specs = (P("row", None), P("row", "col"), P("col"))
    out_specs = (P("row", "col"), P("row", "col"))
    return jax.shard_map(shards, mesh=mesh, in_specs=in_specs, out_specs=out_specs, check_vma=False)
```

```python
import functools

import jax
import jax.numpy as jnp
from jax import lax
from jax.experimental import pallas as pl
from jax.experimental.pallas import tpu as pltpu
from jax.sharding import PartitionSpec as P

step_rate = 0.5
epsilon = 1e-06
f32 = jnp.float32
bf16 = jnp.bfloat16


def dot_nn(a, b):
    return lax.dot_general(a, b, (((1,), (0,)), ((), ())), preferred_element_type=f32)


def dot_nt(a, b):
    return lax.dot_general(a, b, (((1,), (1,)), ((), ())), preferred_element_type=f32)


def dot_tn(a, b):
    return lax.dot_general(a, b, (((0,), (0,)), ((), ())), preferred_element_type=f32)


def swap(x, by):
    return lax.ppermute(x, "row", [(i, i ^ by) for i in range(4)])


def gram_kernel(count, own, mate, far, far_mate, out, act, acc, send, recv, load_sem, send_sem, recv_sem):
    r = lax.axis_index("row")
    c = lax.axis_index("col")
    rows = own.shape[0]
    half = rows // 2
    piece, width = send.shape[2], send.shape[3]
    bits = [1 << i for i in range(count.bit_length() - 1)]
    orders = (bits, bits[1:2] + bits[:1] + bits[2:])

    loads = [pltpu.make_async_copy(src, act.at[i], load_sem.at[i]) for i, src in enumerate((own, mate, far, far_mate))]
    for load in loads:
        load.start()

    def bit_of(bit):
        return (c // bit) % 2

    def partner(bit):
        return c + bit - 2 * bit * bit_of(bit)

    barrier = pltpu.get_barrier_semaphore()
    for bit in bits:
        pl.semaphore_signal(barrier, inc=1, device_id=(partner(bit), r), device_id_type=pl.DeviceIdType.MESH)
    pl.semaphore_wait(barrier, len(bits))
    for load in loads:
        load.wait()

    odd = r % 2
    last = r // 3
    lhs2 = 3 * last
    rhs2 = (1 - odd) + 3 * odd * (1 - last)
    low = r // 2
    lhs3 = 2 * low
    rhs3 = 2 * (1 - low)
    tile = 256

    def compute(first, stop):
        for col in range(first, stop, tile):
            if col < rows:
                a, b, at = 0, 0, col
            elif col < 2 * rows:
                a, b, at = lhs2, rhs2, col - rows
            else:
                a, b, at = lhs3, rhs3, low * half + (col - 2 * rows)
            right = act[b, pl.ds(pl.multiple_of(at, tile), tile), :]

            @pl.loop(0, rows // tile)
            def _(i):
                at_row = pl.ds(pl.multiple_of(i * tile, tile), tile)
                acc[at_row, col : col + tile] = dot_nt(act[a, at_row, :], right)

    def copy(chain, step, j, group):
        slot = count - (count >> step) + j
        return pltpu.make_async_remote_copy(
            src_ref=send.at[chain, group],
            dst_ref=recv.at[chain, slot],
            send_sem=send_sem.at[chain, slot],
            recv_sem=recv_sem.at[chain, slot],
            device_id=(partner(orders[chain][step]), r),
            device_id_type=pl.DeviceIdType.MESH,
        )

    def group_of(chain, step, j, flip):
        order = orders[chain]
        group = 0
        for bit in order[:step]:
            group = group + bit * bit_of(bit)
        here = bit_of(order[step])
        group = group + order[step] * ((1 - here) if flip else here)
        free = order[step + 1 :]
        for i, bit in enumerate(reversed(free)):
            group = group + bit * ((j // (1 << i)) % 2)
        return group

    def place(chain, group):
        return (pl.ds(pl.multiple_of(group * piece, piece), piece), slice(chain * width, (chain + 1) * width))

    def take(chain, step, j):
        group = group_of(chain, step, j, False)
        copy(chain, step, j, group).wait_recv()
        at = place(chain, group)
        acc[at] += recv[chain, count - (count >> step) + j].astype(f32)

    def step_out(chain, step):
        many = count >> (step + 1)

        @pl.loop(0, many)
        def _(j):
            if step:
                take(chain, step - 1, (1 - bit_of(orders[chain][step])) * many + j)
            group = group_of(chain, step, j, True)
            send[chain, group] = acc[place(chain, group)].astype(bf16)
            copy(chain, step, j, group).start()

    def step_in(chain, step):
        many = count >> (step + 1)

        @pl.loop(0, many)
        def _(j):
            take(chain, step - 1, bit_of(orders[chain][step]) * many + j)

    steps = len(bits)
    for chain in (0, 1):
        compute(chain * width, (chain + 1) * width)
        step_out(chain, 0)
    for step in range(1, steps):
        for chain in (0, 1):
            step_out(chain, step)
        for chain in (0, 1):
            step_in(chain, step)
    for chain in (0, 1):
        take(chain, steps - 1, 0)
        at = place(chain, c)
        out[:, chain * width : (chain + 1) * width] = acc[at].astype(bf16)
    for chain in (0, 1):
        for step in range(steps):

            @pl.loop(0, count >> (step + 1))
            def _(j):
                copy(chain, step, j, group_of(chain, step, j, True)).wait_send()


def gram_sum(own, mate, far, far_mate, count):
    rows, depth = own.shape
    total = 5 * rows // 2
    piece = rows // count
    width = total // 2
    return pl.pallas_call(
        functools.partial(gram_kernel, count),
        out_shape=jax.ShapeDtypeStruct((piece, total), bf16),
        in_specs=[pl.BlockSpec(memory_space=pl.ANY)] * 4,
        out_specs=pl.BlockSpec(memory_space=pltpu.VMEM),
        scratch_shapes=[
            pltpu.VMEM((4, rows, depth), bf16),
            pltpu.VMEM((rows, total), f32),
            pltpu.VMEM((2, count, piece, width), bf16),
            pltpu.VMEM((2, count - 1, piece, width), bf16),
            pltpu.SemaphoreType.DMA((4,)),
            pltpu.SemaphoreType.DMA((2, count - 1)),
            pltpu.SemaphoreType.DMA((2, count - 1)),
        ],
        compiler_params=pltpu.CompilerParams(
            collective_id=0, has_side_effects=True, vmem_limit_bytes=56 * 1024 * 1024
        ),
        cost_estimate=pl.CostEstimate(
            flops=2 * rows * total * depth, bytes_accessed=8 * rows * depth, transcendentals=0
        ),
    )(own, mate, far, far_mate)


def shards(q_left, grad, q_right):
    rows, order = q_left.shape
    r = lax.axis_index("row")
    c = lax.axis_index("col")
    col_count = lax.axis_size("col")
    assert lax.axis_size("row") == 4
    piece = rows // col_count
    width = order // col_count

    q_far_piece = swap(lax.dynamic_slice_in_dim(q_left, c * piece, piece, 0), 2)
    q_far = lax.all_gather(q_far_piece, "col", axis=0, tiled=True)
    grad_far = swap(grad, 2)
    grad_mate = swap(grad, 1)
    grad_far_mate = swap(grad_far, 1)
    grad_all = jnp.zeros((order,) + grad.shape[1:], grad.dtype)
    for by, block in ((0, grad), (1, grad_mate), (2, grad_far), (3, grad_far_mate)):
        grad_all = lax.dynamic_update_slice_in_dim(grad_all, block, (r ^ by) * rows, 0)
    q_mate = swap(q_left, 1)
    q_far_mate = swap(q_far, 1)

    def act_of(q):
        return (dot_nn(q, grad_all) * q_right[None, :]).astype(bf16)

    own = act_of(q_left)
    mate = swap(own, 1)
    far = act_of(q_far)
    far_mate = swap(far, 1)

    own_f = own.astype(f32)
    total_sq = jnp.sum(own_f * own_f).reshape(1, 1)
    total_sq = total_sq + swap(total_sq, 1)
    total_sq = total_sq + swap(total_sq, 2)
    by = 1
    while by < col_count:
        total_sq = total_sq + lax.ppermute(total_sq, "col", [(i, i ^ by) for i in range(col_count)])
        by *= 2
    scale = total_sq / order + epsilon

    even = (r % 2) == 0
    gram = gram_sum(own, mate, far, far_mate, col_count)
    p1 = gram[:, :rows]
    p2 = gram[:, rows : 2 * rows]
    p3 = gram[:, 2 * rows :]
    got3 = lax.ppermute(p3, "row", [(2, 0), (3, 1)])
    got2 = lax.ppermute(p2, "row", [(3, 0)])
    zero = jnp.zeros_like(p1)
    row_ids = c * piece + lax.broadcasted_iota(jnp.int32, p1.shape, 0)
    col_ids = lax.broadcasted_iota(jnp.int32, p1.shape, 1)
    upper = jnp.concatenate(
        [
            jnp.where(col_ids >= row_ids, p1, zero),
            jnp.where(even, p2, zero),
            jnp.where(r < 2, jnp.concatenate([p3, got3], axis=1), zero),
            jnp.where(r == 0, got2, jnp.where(r == 1, p2, zero)),
        ],
        axis=1,
    )
    q_all = jnp.concatenate([q_left, q_mate, q_far, q_far_mate], axis=0)
    ratio = (dot_nn(upper, q_all) / scale).astype(bf16)
    ratio = lax.all_to_all(ratio, "col", split_axis=1, concat_axis=0, tiled=True)
    q_tile = lax.dynamic_slice_in_dim(q_left, c * width, width, 1).astype(f32)
    new_left = q_tile - step_rate * (ratio.astype(f32) - q_tile)
    q_cols = lax.dynamic_slice_in_dim(q_all, r * rows, rows, 1)
    act_all = jnp.concatenate([own, mate, far, far_mate], axis=0)
    precond = (dot_tn(q_cols, act_all) * q_right[None, :]).astype(bf16)
    return (new_left, precond)


def solution(mesh):
    in_specs = (P("row", None), P("row", "col"), P("col"))
    out_specs = (P("row", "col"), P("row", "col"))
    return jax.shard_map(shards, mesh=mesh, in_specs=in_specs, out_specs=out_specs, check_vma=False)
```

```python
import functools

import jax
import jax.numpy as jnp
from jax import lax
from jax.experimental import pallas as pl
from jax.experimental.pallas import tpu as pltpu
from jax.sharding import PartitionSpec as P

step_rate = 0.5
epsilon = 1e-06
f32 = jnp.float32
bf16 = jnp.bfloat16


def dot_nn(a, b):
    return lax.dot_general(a, b, (((1,), (0,)), ((), ())), preferred_element_type=f32)


def dot_nt(a, b):
    return lax.dot_general(a, b, (((1,), (1,)), ((), ())), preferred_element_type=f32)


def dot_tn(a, b):
    return lax.dot_general(a, b, (((0,), (0,)), ((), ())), preferred_element_type=f32)


def swap(x, by):
    return lax.ppermute(x, "row", [(i, i ^ by) for i in range(4)])


def gram_kernel(count, own, mate, far, far_mate, out, act_out, act, acc, send, recv, load_sem, store_sem, send_sem, recv_sem):
    r = lax.axis_index("row")
    c = lax.axis_index("col")
    rows = own.shape[0]
    half = rows // 2
    piece, width = send.shape[2], send.shape[3]
    bits = [1 << i for i in range(count.bit_length() - 1)]
    orders = (bits, bits[1:2] + bits[:1] + bits[2:])

    loads = [pltpu.make_async_copy(src, act.at[i], load_sem.at[i]) for i, src in enumerate((own, mate, far, far_mate))]
    for load in loads:
        load.start()

    def bit_of(bit):
        return (c // bit) % 2

    def partner(bit):
        return c + bit - 2 * bit * bit_of(bit)

    barrier = pltpu.get_barrier_semaphore()
    for bit in bits:
        pl.semaphore_signal(barrier, inc=1, device_id=(partner(bit), r), device_id_type=pl.DeviceIdType.MESH)
    pl.semaphore_wait(barrier, len(bits))
    for load in loads:
        load.wait()
    stores = [pltpu.make_async_copy(act.at[i], act_out.at[i], store_sem.at[i]) for i in range(4)]
    for store in stores:
        store.start()

    odd = r % 2
    last = r // 3
    lhs2 = 3 * last
    rhs2 = (1 - odd) + 3 * odd * (1 - last)
    low = r // 2
    lhs3 = 2 * low
    rhs3 = 2 * (1 - low)
    tile = 256

    def compute(first, stop):
        for col in range(first, stop, tile):
            if col < rows:
                a, b, at = 0, 0, col
            elif col < 2 * rows:
                a, b, at = lhs2, rhs2, col - rows
            else:
                a, b, at = lhs3, rhs3, low * half + (col - 2 * rows)
            right = act[b, pl.ds(pl.multiple_of(at, tile), tile), :]

            @pl.loop(0, rows // tile)
            def _(i):
                at_row = pl.ds(pl.multiple_of(i * tile, tile), tile)
                acc[at_row, col : col + tile] = dot_nt(act[a, at_row, :], right)

    def copy(chain, step, j, group):
        slot = count - (count >> step) + j
        return pltpu.make_async_remote_copy(
            src_ref=send.at[chain, group],
            dst_ref=recv.at[chain, slot],
            send_sem=send_sem.at[chain, slot],
            recv_sem=recv_sem.at[chain, slot],
            device_id=(partner(orders[chain][step]), r),
            device_id_type=pl.DeviceIdType.MESH,
        )

    def group_of(chain, step, j, flip):
        order = orders[chain]
        group = 0
        for bit in order[:step]:
            group = group + bit * bit_of(bit)
        here = bit_of(order[step])
        group = group + order[step] * ((1 - here) if flip else here)
        free = order[step + 1 :]
        for i, bit in enumerate(reversed(free)):
            group = group + bit * ((j // (1 << i)) % 2)
        return group

    def place(chain, group):
        return (pl.ds(pl.multiple_of(group * piece, piece), piece), slice(chain * width, (chain + 1) * width))

    def take(chain, step, j):
        group = group_of(chain, step, j, False)
        copy(chain, step, j, group).wait_recv()
        at = place(chain, group)
        acc[at] += recv[chain, count - (count >> step) + j].astype(f32)

    def step_out(chain, step):
        many = count >> (step + 1)

        @pl.loop(0, many)
        def _(j):
            if step:
                take(chain, step - 1, (1 - bit_of(orders[chain][step])) * many + j)
            group = group_of(chain, step, j, True)
            send[chain, group] = acc[place(chain, group)].astype(bf16)
            copy(chain, step, j, group).start()

    def step_in(chain, step):
        many = count >> (step + 1)

        @pl.loop(0, many)
        def _(j):
            take(chain, step - 1, bit_of(orders[chain][step]) * many + j)

    steps = len(bits)
    for chain in (0, 1):
        compute(chain * width, (chain + 1) * width)
        step_out(chain, 0)
    for step in range(1, steps):
        for chain in (0, 1):
            step_out(chain, step)
        for chain in (0, 1):
            step_in(chain, step)
    for chain in (0, 1):
        take(chain, steps - 1, 0)
        at = place(chain, c)
        out[:, chain * width : (chain + 1) * width] = acc[at].astype(bf16)
    for chain in (0, 1):
        for step in range(steps):

            @pl.loop(0, count >> (step + 1))
            def _(j):
                copy(chain, step, j, group_of(chain, step, j, True)).wait_send()

    for store in stores:
        store.wait()


def gram_sum(own, mate, far, far_mate, count):
    rows, depth = own.shape
    total = 5 * rows // 2
    piece = rows // count
    width = total // 2
    return pl.pallas_call(
        functools.partial(gram_kernel, count),
        out_shape=(
            jax.ShapeDtypeStruct((piece, total), bf16),
            jax.ShapeDtypeStruct((4, rows, depth), bf16),
        ),
        in_specs=[pl.BlockSpec(memory_space=pl.ANY)] * 4,
        out_specs=(pl.BlockSpec(memory_space=pltpu.VMEM), pl.BlockSpec(memory_space=pl.ANY)),
        scratch_shapes=[
            pltpu.VMEM((4, rows, depth), bf16),
            pltpu.VMEM((rows, total), f32),
            pltpu.VMEM((2, count, piece, width), bf16),
            pltpu.VMEM((2, count - 1, piece, width), bf16),
            pltpu.SemaphoreType.DMA((4,)),
            pltpu.SemaphoreType.DMA((4,)),
            pltpu.SemaphoreType.DMA((2, count - 1)),
            pltpu.SemaphoreType.DMA((2, count - 1)),
        ],
        compiler_params=pltpu.CompilerParams(
            collective_id=0, has_side_effects=True, vmem_limit_bytes=56 * 1024 * 1024
        ),
        cost_estimate=pl.CostEstimate(
            flops=2 * rows * total * depth, bytes_accessed=8 * rows * depth, transcendentals=0
        ),
    )(own, mate, far, far_mate)


def shards(q_left, grad, q_right):
    rows, order = q_left.shape
    r = lax.axis_index("row")
    c = lax.axis_index("col")
    col_count = lax.axis_size("col")
    assert lax.axis_size("row") == 4
    piece = rows // col_count
    width = order // col_count

    q_far_piece = swap(lax.dynamic_slice_in_dim(q_left, c * piece, piece, 0), 2)
    q_far = lax.all_gather(q_far_piece, "col", axis=0, tiled=True)
    grad_far = swap(grad, 2)
    grad_mate = swap(grad, 1)
    grad_far_mate = swap(grad_far, 1)
    grad_all = jnp.zeros((order,) + grad.shape[1:], grad.dtype)
    for by, block in ((0, grad), (1, grad_mate), (2, grad_far), (3, grad_far_mate)):
        grad_all = lax.dynamic_update_slice_in_dim(grad_all, block, (r ^ by) * rows, 0)
    q_mate = swap(q_left, 1)
    q_far_mate = swap(q_far, 1)

    def act_of(q):
        return (dot_nn(q, grad_all) * q_right[None, :]).astype(bf16)

    own = act_of(q_left)
    mate = swap(own, 1)
    far = act_of(q_far)
    far_mate = swap(far, 1)

    own_f = own.astype(f32)
    total_sq = jnp.sum(own_f * own_f).reshape(1, 1)
    total_sq = total_sq + swap(total_sq, 1)
    total_sq = total_sq + swap(total_sq, 2)
    by = 1
    while by < col_count:
        total_sq = total_sq + lax.ppermute(total_sq, "col", [(i, i ^ by) for i in range(col_count)])
        by *= 2
    scale = total_sq / order + epsilon

    even = (r % 2) == 0
    gram, act_all = gram_sum(own, mate, far, far_mate, col_count)
    p1 = gram[:, :rows]
    p2 = gram[:, rows : 2 * rows]
    p3 = gram[:, 2 * rows :]
    got3 = lax.ppermute(p3, "row", [(2, 0), (3, 1)])
    got2 = lax.ppermute(p2, "row", [(3, 0)])
    zero = jnp.zeros_like(p1)
    row_ids = c * piece + lax.broadcasted_iota(jnp.int32, p1.shape, 0)
    col_ids = lax.broadcasted_iota(jnp.int32, p1.shape, 1)
    upper = [
        jnp.where(col_ids >= row_ids, p1, zero),
        jnp.where(even, p2, zero),
        jnp.where(r < 2, jnp.concatenate([p3, got3], axis=1), zero),
        jnp.where(r == 0, got2, jnp.where(r == 1, p2, zero)),
    ]
    q_rows = (q_left, q_mate, q_far, q_far_mate)
    stepped = sum(dot_nn(u, q) for u, q in zip(upper, q_rows))
    ratio = (stepped / scale).astype(bf16)
    ratio = lax.all_to_all(ratio, "col", split_axis=1, concat_axis=0, tiled=True)
    q_tile = lax.dynamic_slice_in_dim(q_left, c * width, width, 1).astype(f32)
    new_left = q_tile - step_rate * (ratio.astype(f32) - q_tile)
    q_cols = jnp.concatenate([lax.dynamic_slice_in_dim(q, r * rows, rows, 1) for q in q_rows], axis=0)
    act_all = act_all.reshape(order, grad.shape[1])
    precond = (dot_tn(q_cols, act_all) * q_right[None, :]).astype(bf16)
    return (new_left, precond)


def solution(mesh):
    in_specs = (P("row", None), P("row", "col"), P("col"))
    out_specs = (P("row", "col"), P("row", "col"))
    return jax.shard_map(shards, mesh=mesh, in_specs=in_specs, out_specs=out_specs, check_vma=False)
```
